32 devices in a mesh: cells: 8 (over z, y), grp: 4 (over x, core).
Axes of the slice: x: 2, y: 2, z: 4, core: 2. Of those that a mesh axis runs over, the one named last changes fastest.
Arguments:
- positions: float32 [3, 256, 512], P(None, ('cells', 'grp')), may hold values from 0 to 1
- velocities: float32 [3, 256, 512], P(None, ('cells', 'grp')), may hold values from -4 to 4
- smoothing: float32 [256, 512], P(('cells', 'grp')), may hold values from 0.19 to 0.2
- masses: float32 [256, 512], P(('cells', 'grp')), may hold values from 0.0009765625 to 0.00390625
- entropy: float32 [256, 512], P(('cells', 'grp')), may hold values from 0.5 to 2
- density_old: float32 [256, 512], P(('cells', 'grp')), may hold values from 0.5 to 1.5
- active_rows: int32 [256, 64], P(('cells', 'grp')), may hold values from 0 to 511, as said below
- pairs: int32 [3328, 5], P(('cells', 'grp')), may hold values from 0 to 26, as said below
Outputs:
- density_active: float32 [256, 64], P(('cells', 'grp'))
- acceleration: float32 [3, 256, 64], P(None, ('cells', 'grp'))
The draws below stay inside these ranges and needn't reach their ends.
Inputs may be any that keep to these rules, and one draw needn't show every extreme that they name: `active_rows`: each row holds 64 different particle indices of its cell in increasing order. A row of pairs holds (a, s, q, c, k): the home cell a among the 8 cells of the device holding the row, s = 0 for a far cell on the same index of cells or 1 for the next index (cyclically), the grp index q of the far cell's device, its cell c among that device's 8 cells, and the image code k, which is never 13.
All inputs are finite; a program needn't handle non-finite values.
Results may differ from the reference program's by a relative error of at most 0.0003.
Values sent between devices are 32-bit elements; how exact they have to be, the bound alone decides.
A program may use at most 64 MiB of HBM per device.

```python
import math
import jax
import jax.numpy as jnp
from jax import lax

P_SIZE = 512
ACT = 64
CD = 8
PD = 104
NCELL = 256
NPAIR = 3328
N_CELLS = 8
N_GRP = 4
DEVICES = 32


def draw_active_rows(key, part):
    key = jax.random.fold_in(key, 3)
    keys = jax.random.split(key, NCELL)
    chosen = jax.vmap(lambda single: jnp.sort(jax.random.permutation(single, P_SIZE)[:ACT]))(keys)
    return chosen.astype(jnp.int32)


def draw_pairs(key, part):
    key = jax.random.fold_in(key, 5)
    keys = jax.random.split(key, 5)
    home = jax.random.randint(keys[0], (NPAIR,), 0, CD)
    cycle = jax.random.randint(keys[1], (NPAIR,), 0, 2)
    group = jax.random.randint(keys[2], (NPAIR,), 0, N_GRP)
    cell = jax.random.randint(keys[3], (NPAIR,), 0, CD)
    code = jax.random.randint(keys[4], (NPAIR,), 0, 26)
    code = code + (code >= 13).astype(code.dtype)
    return jnp.stack([home, cycle, group, cell, code], axis=1).astype(jnp.int32)


def block_levels(stream_key, shape, cuts, low, top_value):
    def one(axis_at, shards_of):
        steps = jax.random.uniform(jax.random.fold_in(jax.random.fold_in(stream_key, 6), axis_at), (shards_of,), jnp.float32, low / len(cuts), top_value / len(cuts))
        return jnp.repeat(jnp.exp(steps), shape[axis_at] // shards_of).reshape((-1,) + (1,) * (len(shape) - axis_at - 1))

    gain = one(*cuts[0])
    for cut in cuts[1:]:
        gain = gain * one(*cut)
    return gain


def bell_draw(rng, shape, width, reach, cuts=(), kind=jnp.bfloat16):
    entries = jax.random.normal(rng, shape, jnp.float32) * width
    if len(cuts) > 0:
        entries = block_levels(rng, shape, cuts, -0.22, 0.18) * entries
    return jnp.clip(entries, min=-reach, max=reach).astype(kind)


def setup_inputs(seed: int = 0) -> dict:
    splits = jax.random.split(jax.random.key(seed), 9)
    positions = jnp.clip(1.0 * jax.random.uniform(splits[0], (3, NCELL, P_SIZE), jnp.float32) ** block_levels(splits[0], (3, NCELL, P_SIZE), ((1, 32),), -0.2, 0.2), 0.0, 1.0)
    velocities = bell_draw(splits[1], (3, NCELL, P_SIZE), 1.0, 4.0, ((1, 32),), jnp.float32)
    smoothing = jnp.clip(jnp.exp(math.log(0.2) - 0.05129332 * jax.random.uniform(splits[2], (NCELL, P_SIZE), jnp.float32) ** block_levels(splits[2], (NCELL, P_SIZE), ((0, 32),), -0.2, 0.2)), 0.19, 0.2)
    masses = jnp.clip(jnp.exp(math.log(0.00390625) - 1.3862944 * jax.random.uniform(splits[3], (NCELL, P_SIZE), jnp.float32) ** block_levels(splits[3], (NCELL, P_SIZE), ((0, 32),), -0.2, 0.2)), 0.0009765625, 0.00390625)
    entropy = jnp.clip(jnp.exp(math.log(2.0) - 1.3862944 * jax.random.uniform(splits[4], (NCELL, P_SIZE), jnp.float32) ** block_levels(splits[4], (NCELL, P_SIZE), ((0, 32),), -0.2, 0.2)), 0.5, 2.0)
    density_old = jnp.clip(0.5 + 1.0 * jax.random.uniform(splits[5], (NCELL, P_SIZE), jnp.float32) ** block_levels(splits[5], (NCELL, P_SIZE), ((0, 32),), -0.2, 0.2), 0.5, 1.5)
    active_rows = draw_active_rows(jax.random.fold_in(splits[8], 71), 0)
    pairs = draw_pairs(jax.random.fold_in(splits[8], 71), 0)
    return {"positions": positions, "velocities": velocities, "smoothing": smoothing, "masses": masses, "entropy": entropy, "density_old": density_old, "active_rows": active_rows, "pairs": pairs}


GAMMA = 5.0 / 3.0
ALPHA_VISC = 1.0
BETA_VISC = 2.0

def kernel_value(dist2, smooth):
    q = jnp.sqrt(dist2) / smooth
    inner = 1.0 - 1.5 * q * q + 0.75 * q * q * q
    outer = 0.25 * jnp.maximum(2.0 - q, 0.0) ** 3
    return jnp.where(q < 1.0, inner, outer) / (jnp.pi * smooth ** 3)

def kernel_slope(dist2, smooth):
    q = jnp.sqrt(dist2) / smooth
    inner = -3.0 + 2.25 * q
    outer = -0.75 * jnp.maximum(2.0 - q, 0.0) ** 2 / jnp.maximum(q, 1.0)
    return jnp.where(q < 1.0, inner, outer) / (jnp.pi * smooth ** 5)

def density_terms(pos_i, smooth_i, pos_j, mass_j):
    sep = pos_i[:, :, :, None] - pos_j[:, :, None, :]
    dist2 = lax.optimization_barrier(jnp.sum(sep * sep, axis=1))
    return lax.optimization_barrier(jnp.sum(mass_j[:, None, :] * kernel_value(dist2, smooth_i[:, :, None]), axis=2))

def force_terms(side_i, side_j):
    pos_i, vel_i, smooth_i, press_i, rho_i, sound_i = side_i
    pos_j, vel_j, smooth_j, press_j, rho_j, sound_j, mass_j = side_j
    sep = pos_i[:, :, :, None] - pos_j[:, :, None, :]
    vsep = vel_i[:, :, :, None] - vel_j[:, :, None, :]
    dist2 = lax.optimization_barrier(jnp.sum(sep * sep, axis=1))
    approach = lax.optimization_barrier(jnp.sum(sep * vsep, axis=1))
    smooth = 0.5 * (smooth_i[:, :, None] + smooth_j[:, None, :])
    motion = smooth * jnp.minimum(approach, 0.0) / (dist2 + 0.01 * smooth * smooth)
    sound = 0.5 * (sound_i[:, :, None] + sound_j[:, None, :])
    visc = (-ALPHA_VISC * sound * motion + BETA_VISC * motion * motion) / (0.5 * (rho_i[:, :, None] + rho_j[:, None, :]))
    coef = mass_j[:, None, :] * (press_i[:, :, None] + press_j[:, None, :] + visc) * kernel_slope(dist2, smooth)
    return -lax.optimization_barrier(jnp.sum(coef[:, None, :, :] * sep, axis=3))

def reference(positions, velocities, smoothing, masses, entropy, density_old, active_rows, pairs):
    cell_pos = jnp.transpose(positions, (1, 0, 2))
    cell_vel = jnp.transpose(velocities, (1, 0, 2))
    choose = active_rows[:, None, :]
    act_pos = jnp.take_along_axis(cell_pos, choose, axis=2)
    act_vel = jnp.take_along_axis(cell_vel, choose, axis=2)
    act_smooth = jnp.take_along_axis(smoothing, active_rows, axis=1)
    act_entropy = jnp.take_along_axis(entropy, active_rows, axis=1)
    rows = jnp.arange(NPAIR, dtype=jnp.int32)
    device = rows // PD
    home = device * CD + pairs[:, 0]
    cycle = device // N_GRP
    far = ((cycle + pairs[:, 1]) % N_CELLS * N_GRP + pairs[:, 2]) * CD + pairs[:, 3]
    code = pairs[:, 4]
    offset = jnp.stack([code // 9 - 1, code // 3 % 3 - 1, code % 3 - 1], axis=1).astype(jnp.float32)
    blocks = NPAIR // CD
    stacked = (home.reshape(blocks, CD), far.reshape(blocks, CD), offset.reshape(blocks, CD, 3))

    def density_step(total, block):
        here, there, moved = block
        own_part = density_terms(act_pos[here], act_smooth[here], cell_pos[there] + moved[:, :, None], masses[there])
        far_part = density_terms(act_pos[there] - moved[:, :, None], act_smooth[there], cell_pos[here], masses[here])
        return (total.at[here].add(own_part).at[there].add(far_part), None)
    pair_rho, _ = lax.scan(density_step, jnp.zeros((NCELL, ACT), jnp.float32), stacked)
    self_rho = lax.map(lambda block: density_terms(block[0], block[1], block[2], block[3]), (act_pos.reshape(DEVICES, CD, 3, ACT), act_smooth.reshape(DEVICES, CD, ACT), cell_pos.reshape(DEVICES, CD, 3, P_SIZE), masses.reshape(DEVICES, CD, P_SIZE))).reshape(NCELL, ACT)
    rho_act = self_rho + pair_rho
    rho_full = density_old.at[jnp.arange(NCELL, dtype=jnp.int32)[:, None], active_rows].set(rho_act)
    press_full = entropy * rho_full ** (-1.0 / 3.0)
    sound_full = jnp.sqrt(GAMMA * entropy) * rho_full ** (1.0 / 3.0)
    press_act = act_entropy * rho_act ** (-1.0 / 3.0)
    sound_act = jnp.sqrt(GAMMA * act_entropy) * rho_act ** (1.0 / 3.0)

    def force_step(total, block):
        here, there, moved = block
        own_part = force_terms((act_pos[here], act_vel[here], act_smooth[here], press_act[here], rho_act[here], sound_act[here]), (cell_pos[there] + moved[:, :, None], cell_vel[there], smoothing[there], press_full[there], rho_full[there], sound_full[there], masses[there]))
        far_part = force_terms((act_pos[there] - moved[:, :, None], act_vel[there], act_smooth[there], press_act[there], rho_act[there], sound_act[there]), (cell_pos[here], cell_vel[here], smoothing[here], press_full[here], rho_full[here], sound_full[here], masses[here]))
        return (total.at[here].add(own_part).at[there].add(far_part), None)
    pair_acc, _ = lax.scan(force_step, jnp.zeros((NCELL, 3, ACT), jnp.float32), stacked)

    def self_force(block):
        return force_terms(block[:6], block[6:])
    self_acc = lax.map(self_force, (act_pos.reshape(DEVICES, CD, 3, ACT), act_vel.reshape(DEVICES, CD, 3, ACT), act_smooth.reshape(DEVICES, CD, ACT), press_act.reshape(DEVICES, CD, ACT), rho_act.reshape(DEVICES, CD, ACT), sound_act.reshape(DEVICES, CD, ACT), cell_pos.reshape(DEVICES, CD, 3, P_SIZE), cell_vel.reshape(DEVICES, CD, 3, P_SIZE), smoothing.reshape(DEVICES, CD, P_SIZE), press_full.reshape(DEVICES, CD, P_SIZE), rho_full.reshape(DEVICES, CD, P_SIZE), sound_full.reshape(DEVICES, CD, P_SIZE), masses.reshape(DEVICES, CD, P_SIZE))).reshape(NCELL, 3, ACT)
    acceleration = jnp.transpose(self_acc + pair_acc, (1, 0, 2))
    return (rho_act, acceleration)
```

```python
import functools
import math

import jax
import jax.numpy as jnp
from jax import lax
from jax.experimental import pallas as pl
from jax.experimental.pallas import tpu as pltpu
from jax.sharding import PartitionSpec as P

GAMMA = 5.0 / 3.0
HIGHEST = lax.Precision.HIGHEST
REACH2 = 0.1601
LANES = 128
FAR_WORD = (3 << 18) | (3 << 20) | (3 << 22)
MESH = pl.DeviceIdType.MESH
VMEM = pl.BlockSpec(memory_space=pltpu.VMEM)
SMEM = pl.BlockSpec(memory_space=pltpu.SMEM)
ANY = pl.BlockSpec(memory_space=pl.ANY)
CONTRACT = (((1,), (1,)), ((), ()))


def partners(n_cells, n_grp):
    me_c, me_g = lax.axis_index("cells"), lax.axis_index("grp")
    out = []
    for step in (0, 1, -1):
        for turn in range(n_grp):
            if step == 0 and turn == 0:
                continue
            there = (lax.rem(me_c + step + n_cells, n_cells), lax.rem(me_g + turn, n_grp))
            out.append((there, (1 - step) * n_grp + me_g))
    return me_g, out


def greet(others):
    barrier = pltpu.get_barrier_semaphore()
    for there, _ in others:
        pl.semaphore_signal(barrier, inc=1, device_id=there, device_id_type=MESH)
    pl.semaphore_wait(barrier, len(others))


def spread(others, me_slot, pieces, sends, recvs, local_sem):
    copies = []
    count = 0
    for there, slot in others:
        for src, dst in pieces:
            copy = pltpu.make_async_remote_copy(
                src_ref=src,
                dst_ref=dst.at[slot],
                send_sem=sends.at[count],
                recv_sem=recvs.at[count],
                device_id=there,
                device_id_type=MESH,
            )
            copy.start()
            copies.append(copy)
            count += 1
    for index, (src, dst) in enumerate(pieces):
        copy = pltpu.make_async_copy(src, dst.at[me_slot], local_sem.at[index])
        copy.start()
        copies.append(copy)
    return copies


def below(row, col, first):
    return jnp.logical_or(row < col, jnp.logical_and(row == col, first))


def order_active(table, index_col, index_row, act_ref, arow_ref, rank_ref, mask_ref, e):
    width = table.shape[1]
    picked = index_col.shape[0]
    sel = (lax.broadcasted_iota(jnp.int32, (picked, width), 1) == index_col).astype(jnp.float32)
    cols = lax.dot_general(sel, table, CONTRACT, precision=HIGHEST, preferred_element_type=jnp.float32)
    rows = lax.dot_general(table, sel, CONTRACT, precision=HIGHEST, preferred_element_type=jnp.float32)
    ii = lax.broadcasted_iota(jnp.int32, (picked, picked), 0)
    jj = lax.broadcasted_iota(jnp.int32, (picked, picked), 1)
    same = jj >= 0
    place_c = jnp.zeros((picked, 1), jnp.float32)
    place_r = jnp.zeros((1, picked), jnp.float32)
    size = picked
    for axis in range(3):
        col, row = cols[:, axis : axis + 1], rows[axis : axis + 1, :]
        in_col = jnp.logical_and(same, below(row, col, jj < ii))
        in_row = jnp.logical_and(same, below(col, row, ii < jj))
        rank_c = jnp.sum(jnp.where(in_col, 1.0, 0.0), axis=1, keepdims=True)
        rank_r = jnp.sum(jnp.where(in_row, 1.0, 0.0), axis=0, keepdims=True)
        if axis == 2:
            place_c = place_c + rank_c
            place_r = place_r + rank_r
            break
        size //= 2
        half_c = jnp.where(rank_c >= size, float(size), 0.0)
        half_r = jnp.where(rank_r >= size, float(size), 0.0)
        place_c = place_c + half_c
        place_r = place_r + half_r
        same = jnp.logical_and(same, half_c == half_r)
    perm = (ii.astype(jnp.float32) == place_r).astype(jnp.float32)
    ordered = lax.dot_general(
        perm, cols, (((1,), (0,)), ((), ())), precision=HIGHEST, preferred_element_type=jnp.float32
    )
    act_ref[e] = ordered
    arow_ref[e] = jnp.sum(perm * index_row.astype(jnp.float32), axis=1, keepdims=True).astype(jnp.int32)
    rank_ref[e] = place_r
    boxes = ordered.reshape(picked // 8, 8, ordered.shape[1])
    low, high = jnp.min(boxes, axis=1), jnp.max(boxes, axis=1)
    code = lax.broadcasted_iota(jnp.int32, (picked // 8, LANES), 1).astype(jnp.float32)
    top = jnp.where(code >= 9.0, 1.0, 0.0) + jnp.where(code >= 18.0, 1.0, 0.0)
    rest = code - 9.0 * top
    mid = jnp.where(rest >= 3.0, 1.0, 0.0) + jnp.where(rest >= 6.0, 1.0, 0.0)
    apart = jnp.zeros_like(code)
    for axis, shift in enumerate((top - 1.0, mid - 1.0, rest - 3.0 * mid - 1.0)):
        gap = jnp.maximum(low[:, axis : axis + 1] - (shift + 1.0), shift - high[:, axis : axis + 1])
        gap = jnp.maximum(gap, 0.0)
        apart = apart + gap * gap
    bit = jnp.left_shift(1, lax.broadcasted_iota(jnp.int32, (picked // 8, LANES), 0)).astype(jnp.float32)
    mask_ref[e] = jnp.sum(jnp.where(apart < REACH2, bit, 0.0), axis=0, keepdims=True).astype(jnp.int32)


def first_kernel(
    n_cells, n_grp, table_ref, pairs_ref, icol_ref, irow_ref,
    all_ref, rows_ref, act_ref, arow_ref, rank_ref, mask_ref,
    sends, recvs, local_sem,
):
    me_g, others = partners(n_cells, n_grp)
    greet(others)
    copies = spread(
        others, n_grp + me_g, ((table_ref, all_ref), (pairs_ref, rows_ref)), sends, recvs, local_sem
    )
    for e in range(table_ref.shape[0]):
        order_active(
            table_ref[e], icol_ref[e], irow_ref[e], act_ref, arow_ref, rank_ref, mask_ref, e
        )
    for copy in copies:
        copy.wait()


def second_kernel(n_cells, n_grp, mine_ref, all_ref, sends, recvs, local_sem):
    me_g, others = partners(n_cells, n_grp)
    greet(others)
    for copy in spread(others, n_grp + me_g, ((mine_ref, all_ref),), sends, recvs, local_sem):
        copy.wait()


def unit_shift(word):
    return [((word >> bits) & 3).astype(jnp.float32) - 1.0 for bits in (18, 20, 22)]


def density_kernel(
    words_ref, mask_ref, table_ref, act_ref, arow_ref, rank_ref, entropy_ref, old_ref,
    rho_out, rho_col, press_col, state_out, units_ref, count_ref,
    entries, wide, acc,
):
    cells, picked, _ = act_ref.shape
    width = table_ref.shape[2]
    groups = picked // 8
    total = words_ref.shape[0]

    def keep(step, found):
        for k in range(8):
            word = words_ref[step * 8 + k]
            entries[found] = word
            found = found + (word >> 21)
        return found

    found = lax.fori_loop(0, total // 8, keep, jnp.int32(0))

    def unfold(step, count):
        word = entries[step]
        bits = mask_ref[(word & 7) * LANES + ((word >> 10) & 31)]
        base = (word & 0x1FFFFF) << 3
        for g in range(groups):
            units_ref[count] = base + g
            count = count + ((bits >> g) & 1)
        return count

    count = lax.fori_loop(0, found, unfold, jnp.int32(0))
    for k in range(4):
        units_ref[count + k] = jnp.int32(FAR_WORD)
    count_ref[0] = count

    for e in range(cells):
        data = act_ref[e]
        for f, col in enumerate((data[:, 0:1], data[:, 1:2], data[:, 2:3], 1.0 / (data[:, 6:7] * data[:, 6:7]))):
            wide[f, e * groups : (e + 1) * groups] = jnp.broadcast_to(col, (picked, LANES)).reshape(
                groups, 8, LANES
            )
    acc[...] = jnp.zeros_like(acc)

    def pair(step, carry):
        results = []
        for k in range(2):
            word = units_ref[step * 2 + k]
            ig = word & 63
            far = (word >> 6) & 127
            ox, oy, oz = unit_shift(word)
            xi, yi, zi = wide[0, ig] - ox, wide[1, ig] - oy, wide[2, ig] - oz
            ih2 = wide[3, ig]
            part = None
            for t in range(width // LANES):
                at = pl.ds(t * LANES, LANES)
                dx = xi - table_ref[far, 0:1, at]
                dy = yi - table_ref[far, 1:2, at]
                dz = zi - table_ref[far, 2:3, at]
                q2 = (dx * dx + dy * dy + dz * dz) * ih2
                q = q2 * lax.rsqrt(jnp.maximum(q2, 1e-30))
                u = 1.0 - q
                w = jnp.maximum(u + 1.0, 0.0)
                u = jnp.maximum(u, 0.0)
                value = table_ref[far, 7:8, at] * (0.25 * (w * w * w) - u * u * u)
                part = value if part is None else part + value
            results.append((ig, part))
        for ig, part in results:
            acc[ig] += part
        return carry

    lax.fori_loop(0, (count + 1) // 2, pair, 0)

    ii = lax.broadcasted_iota(jnp.int32, (picked, picked), 0).astype(jnp.float32)
    lane = lax.broadcasted_iota(jnp.int32, (picked, width), 1)
    for e in range(cells):
        h = act_ref[e][:, 6:7]
        col = jnp.sum(acc[e * groups : (e + 1) * groups].reshape(picked, LANES), axis=1, keepdims=True)
        col = col / (math.pi * h * h * h)
        rho_out[e : e + 1, :] = jnp.sum(jnp.where(ii == rank_ref[e], col, 0.0), axis=0, keepdims=True)
        hit = lane == arow_ref[e]
        entropy = entropy_ref[e : e + 1, :]
        placed = jnp.sum(jnp.where(hit, col, 0.0), axis=0, keepdims=True)
        any_hit = jnp.sum(jnp.where(hit, 1.0, 0.0), axis=0, keepdims=True)
        rho = jnp.where(any_hit > 0.0, placed, old_ref[e : e + 1, :])
        own_entropy = jnp.sum(jnp.where(hit, entropy, 0.0), axis=1, keepdims=True)
        state_out[e, 0:1, :] = rho
        state_out[e, 1:2, :] = entropy * jnp.exp(jnp.log(rho) * (-1.0 / 3.0))
        rho_col[e] = col
        press_col[e] = own_entropy * jnp.exp(jnp.log(col) * (-1.0 / 3.0))


def inverse(x):
    y = pl.reciprocal(x, approx=True)
    return y * (2.0 - x * y)


def force_kernel(
    units_ref, count_ref, table_ref, state_ref, act_ref, rho_col, press_col, rank_ref,
    acc_out, wide, acc,
):
    cells, picked, _ = act_ref.shape
    width = table_ref.shape[2]
    groups = picked // 8
    for e in range(cells):
        data = act_ref[e]
        rho, press = rho_col[e], press_col[e]
        sound = 0.5 * jnp.sqrt(GAMMA * press * rho)
        fields = [data[:, f : f + 1] for f in range(6)] + [0.5 * data[:, 6:7], press, rho, sound]
        for f, col in enumerate(fields):
            wide[f, e * groups : (e + 1) * groups] = jnp.broadcast_to(col, (picked, LANES)).reshape(
                groups, 8, LANES
            )
    acc[...] = jnp.zeros_like(acc)

    def pair(step, carry):
        results = []
        for k in range(2):
            word = units_ref[step * 2 + k]
            ig = word & 63
            far = (word >> 6) & 127
            ox, oy, oz = unit_shift(word)
            xi, yi, zi = wide[0, ig] - ox, wide[1, ig] - oy, wide[2, ig] - oz
            ui, vi, wi = wide[3, ig], wide[4, ig], wide[5, ig]
            hi, pi, ri, si = wide[6, ig], wide[7, ig], wide[8, ig], wide[9, ig]
            parts = None
            for t in range(width // LANES):
                at = pl.ds(t * LANES, LANES)
                dx = xi - table_ref[far, 0:1, at]
                dy = yi - table_ref[far, 1:2, at]
                dz = zi - table_ref[far, 2:3, at]
                du = ui - table_ref[far, 3:4, at]
                dv = vi - table_ref[far, 4:5, at]
                dw = wi - table_ref[far, 5:6, at]
                rj, pj = state_ref[far, 0:1, at], state_ref[far, 1:2, at]
                half = GAMMA * 0.25 * (pj * rj)
                sj = half * lax.rsqrt(half)
                r2 = dx * dx + dy * dy + dz * dz
                approach = jnp.minimum(dx * du + dy * dv + dz * dw, 0.0)
                h = hi + 0.5 * table_ref[far, 6:7, at]
                ih = inverse(h)
                ih2 = ih * ih
                q2 = r2 * ih2
                rq = lax.rsqrt(jnp.maximum(q2, 1e-30))
                q = q2 * rq
                w = jnp.maximum(2.0 - q, 0.0)
                slope = jnp.where(q < 1.0, 3.0 - 2.25 * q, 0.75 * (w * w) * rq)
                mu = h * approach * inverse(r2 + 0.01 * (h * h))
                visc = 2.0 * mu * (2.0 * mu - (si + sj)) * inverse(ri + rj)
                coef = (pi + pj + visc) * slope * (ih2 * ih2 * ih) * table_ref[far, 7:8, at]
                new = (coef * dx, coef * dy, coef * dz)
                parts = new if parts is None else tuple(a + b for a, b in zip(parts, new))
            results.append((ig, parts))
        for ig, parts in results:
            for axis in range(3):
                acc[axis, ig] += parts[axis]
        return carry

    lax.fori_loop(0, (count_ref[0] + 1) // 2, pair, 0)
    ii = lax.broadcasted_iota(jnp.int32, (picked, picked), 0).astype(jnp.float32)
    for axis in range(3):
        for e in range(cells):
            col = jnp.sum(
                acc[axis, e * groups : (e + 1) * groups].reshape(picked, LANES), axis=1, keepdims=True
            )
            col = col * (1.0 / math.pi)
            acc_out[axis, e : e + 1, :] = jnp.sum(
                jnp.where(ii == rank_ref[e], col, 0.0), axis=0, keepdims=True
            )


def shape(dims, kind=jnp.float32):
    return jax.ShapeDtypeStruct(dims, kind)


def local(positions, velocities, smoothing, masses, entropy, density_old, active_rows, pairs):
    n_cells, n_grp = lax.axis_size("cells"), lax.axis_size("grp")
    cells, width = smoothing.shape
    picked = active_rows.shape[1]
    listed = pairs.shape[0]
    groups = picked // 8
    slots = 3 * n_grp
    table = jnp.transpose(
        jnp.concatenate([positions, velocities, smoothing[None], masses[None]], axis=0), (1, 0, 2)
    )
    padded = -(-listed // LANES) * LANES
    rows = jnp.pad(pairs.T, ((0, 3), (0, padded - listed)))
    n_copies = slots - 1
    limit = 48 * 1024 * 1024
    far, far_rows, act, arow, rank, mask = pl.pallas_call(
        functools.partial(first_kernel, n_cells, n_grp),
        out_shape=(
            shape((slots, cells, 8, width)),
            shape((slots, 8, padded), jnp.int32),
            shape((cells, picked, 8)),
            shape((cells, picked, 1), jnp.int32),
            shape((cells, 1, picked)),
            shape((cells, 1, LANES), jnp.int32),
        ),
        in_specs=[VMEM] * 4,
        out_specs=(ANY, ANY, VMEM, VMEM, VMEM, VMEM),
        scratch_shapes=[
            pltpu.SemaphoreType.DMA((2 * n_copies,)),
            pltpu.SemaphoreType.DMA((2 * n_copies,)),
            pltpu.SemaphoreType.DMA((2,)),
        ],
        compiler_params=pltpu.CompilerParams(
            collective_id=0, has_side_effects=True, vmem_limit_bytes=limit
        ),
    )(table, rows, active_rows[:, :, None], active_rows[:, None, :])

    me_g = lax.axis_index("grp")

    def word(own, cell, code, valid):
        x, y, z = code // 9, code // 3 % 3, code % 3
        return own | (cell << 3) | (code << 10) | (x << 15) | (y << 17) | (z << 19) | (
            valid.astype(jnp.int32) << 21
        )

    home = word(
        pairs[:, 0],
        ((1 + pairs[:, 1]) * n_grp + pairs[:, 2]) * cells + pairs[:, 3],
        pairs[:, 4],
        jnp.ones((listed,), jnp.bool_),
    )
    seen = far_rows[: 2 * n_grp]
    slot = lax.broadcasted_iota(jnp.int32, (2 * n_grp, listed), 0)
    seen = seen[:, :, :listed]
    ours = (seen[:, 2] == me_g) & (seen[:, 1] == jnp.where(slot < n_grp, 1, 0))
    away = word(seen[:, 3], slot * cells + seen[:, 0], seen[:, 4], ours)
    ids = jnp.arange(cells, dtype=jnp.int32)
    alone = word(ids, (n_grp + me_g) * cells + ids, jnp.full((cells,), 13, jnp.int32), ids >= 0)
    words = jnp.concatenate([home, alone, away.reshape(-1)])
    words = jnp.pad(words, (0, -words.shape[0] % 8))
    n_words = words.shape[0]
    far = far.reshape(slots * cells, 8, width)

    rho_act, rho_col, press_col, state, units, count = pl.pallas_call(
        density_kernel,
        out_shape=(
            shape((cells, picked)),
            shape((cells, picked, 1)),
            shape((cells, picked, 1)),
            shape((cells, 2, width)),
            shape((n_words * groups + 8,), jnp.int32),
            shape((1,), jnp.int32),
        ),
        in_specs=[SMEM, SMEM] + [VMEM] * 6,
        out_specs=(VMEM, VMEM, VMEM, VMEM, SMEM, SMEM),
        scratch_shapes=[
            pltpu.SMEM((n_words + 8,), jnp.int32),
            pltpu.VMEM((4, cells * groups, 8, LANES), jnp.float32),
            pltpu.VMEM((cells * groups, 8, LANES), jnp.float32),
        ],
        compiler_params=pltpu.CompilerParams(vmem_limit_bytes=limit),
    )(words, mask.reshape(-1), far, act, arow, rank, entropy, density_old)

    far_state = pl.pallas_call(
        functools.partial(second_kernel, n_cells, n_grp),
        out_shape=shape((slots, cells, 2, width)),
        in_specs=[VMEM],
        out_specs=ANY,
        scratch_shapes=[
            pltpu.SemaphoreType.DMA((n_copies,)),
            pltpu.SemaphoreType.DMA((n_copies,)),
            pltpu.SemaphoreType.DMA((1,)),
        ],
        compiler_params=pltpu.CompilerParams(collective_id=1, has_side_effects=True),
    )(state).reshape(slots * cells, 2, width)

    acceleration = pl.pallas_call(
        force_kernel,
        out_shape=shape((3, cells, picked)),
        in_specs=[SMEM, SMEM] + [VMEM] * 6,
        out_specs=VMEM,
        scratch_shapes=[
            pltpu.VMEM((10, cells * groups, 8, LANES), jnp.float32),
            pltpu.VMEM((3, cells * groups, 8, LANES), jnp.float32),
        ],
        compiler_params=pltpu.CompilerParams(vmem_limit_bytes=limit),
    )(units, count, far, far_state, act, rho_col, press_col, rank)
    return rho_act, acceleration


def solution(mesh):
    split = ("cells", "grp")
    return jax.shard_map(
        local,
        mesh=mesh,
        in_specs=(
            P(None, split, None),
            P(None, split, None),
            P(split, None),
            P(split, None),
            P(split, None),
            P(split, None),
            P(split, None),
            P(split, None),
        ),
        out_specs=(P(split, None), P(None, split, None)),
        check_vma=False,
    )
```

```python
import functools
import math

import jax
import jax.numpy as jnp
from jax import lax
from jax.experimental import pallas as pl
from jax.experimental.pallas import tpu as pltpu
from jax.sharding import PartitionSpec as P

GAMMA = 5.0 / 3.0
HIGHEST = lax.Precision.HIGHEST
REACH2 = 0.1601
LANES = 128
BATCH = 8
FAR_WORD = (3 << 18) | (3 << 20) | (3 << 22)
MESH = pl.DeviceIdType.MESH
VMEM = pl.BlockSpec(memory_space=pltpu.VMEM)
SMEM = pl.BlockSpec(memory_space=pltpu.SMEM)
ANY = pl.BlockSpec(memory_space=pl.ANY)
CONTRACT = (((1,), (1,)), ((), ()))


def routes(n_cells, n_grp):
    me_c, me_g = lax.axis_index("cells"), lax.axis_index("grp")
    out = []
    for step in (0, 1, -1):
        for turn in range(0, n_grp, 2):
            if step == 0 and turn == 0:
                continue
            there = (lax.rem(me_c + step + n_cells, n_cells), lax.rem(me_g + turn, n_grp))
            base = (1 - step) * n_grp
            out.append((there, base + me_g, base + lax.rem(me_g - turn + n_grp, n_grp)))
    mate = (me_c, me_g + 1 - 2 * lax.rem(me_g, 2))
    return mate, n_grp + me_g, out


def greet(mate, others):
    barrier = pltpu.get_barrier_semaphore()
    for there in [mate] + [other[0] for other in others]:
        pl.semaphore_signal(barrier, inc=1, device_id=there, device_id_type=MESH)
    pl.semaphore_wait(barrier, len(others) + 1)


def remote(src, dst, sends, recvs, index, there):
    copy = pltpu.make_async_remote_copy(
        src_ref=src,
        dst_ref=dst,
        send_sem=sends.at[index],
        recv_sem=recvs.at[index],
        device_id=there,
        device_id_type=MESH,
    )
    copy.start()
    return copy


def spread(mate, mine, others, pieces, sends, recvs, local_sem):
    first, rest = [], []
    count = 0
    for there, slot, _ in others:
        for src, dst in pieces:
            first.append(remote(src, dst.at[slot], sends, recvs, count, there))
            count += 1
    for index, (src, dst) in enumerate(pieces):
        rest.append(remote(src, dst.at[mine], sends, recvs, count, mate))
        count += 1
        copy = pltpu.make_async_copy(src, dst.at[mine], local_sem.at[index])
        copy.start()
        rest.append(copy)
    return first, rest, count


def forward(mate, others, pieces, first, rest, count, sends, recvs):
    at = 0
    for _, _, slot in others:
        for _, dst in pieces:
            first[at].wait_recv()
            rest.append(remote(dst.at[slot], dst.at[slot], sends, recvs, count, mate))
            at += 1
            count += 1
    for copy in first:
        copy.wait_send()
    for copy in rest:
        copy.wait()


def below(row, col, first):
    return jnp.logical_or(row < col, jnp.logical_and(row == col, first))


def code_shifts(rows):
    code = lax.broadcasted_iota(jnp.int32, (rows, LANES), 1).astype(jnp.float32)
    top = jnp.where(code >= 9.0, 1.0, 0.0) + jnp.where(code >= 18.0, 1.0, 0.0)
    rest = code - 9.0 * top
    mid = jnp.where(rest >= 3.0, 1.0, 0.0) + jnp.where(rest >= 6.0, 1.0, 0.0)
    return top - 1.0, mid - 1.0, rest - 3.0 * mid - 1.0


def rank_rows(keys):
    cells, width = keys.shape
    turned = jnp.transpose(keys)
    out = []
    for e in range(cells):
        row = jnp.broadcast_to(keys[e : e + 1, :], (8, width))
        total = jnp.zeros((8, width), jnp.float32)
        for r in range(0, width, 8):
            total = total + jnp.where(turned[r : r + 8, e : e + 1] < row, 1.0, 0.0)
        out.append(jnp.sum(total, axis=0, keepdims=True))
    return jnp.concatenate(out, axis=0)


def tile_order(xs, ys):
    lane = lax.broadcasted_iota(jnp.int32, xs.shape, 1).astype(jnp.float32)
    width = xs.shape[1]
    steps = 8192.0
    half = rank_rows(jnp.floor(xs * steps) * width + lane) >= width // 2
    key = jnp.floor(ys * steps) * width + lane
    return rank_rows(key + jnp.where(half, (steps + 1.0) * width, 0.0))


def split_three(x):
    top = x.astype(jnp.bfloat16)
    rest = x - top.astype(jnp.float32)
    mid = rest.astype(jnp.bfloat16)
    low = (rest - mid.astype(jnp.float32)).astype(jnp.bfloat16)
    return jnp.concatenate([top, mid, low], axis=0)


def permuted(rows, place):
    count, width = rows.shape
    spot = lax.broadcasted_iota(jnp.int32, (width, width), 0).astype(jnp.float32)
    moved = jnp.where(spot == place, 1.0, 0.0).astype(jnp.bfloat16)
    parts = lax.dot_general(split_three(rows), moved, CONTRACT, preferred_element_type=jnp.float32)
    return parts[:count] + parts[count : 2 * count] + parts[2 * count :]


def tile_mask(table):
    row = lax.broadcasted_iota(jnp.int32, (8, LANES), 0)
    sx, sy, sz = code_shifts(8)
    shift = jnp.where(row == 0, sx, jnp.where(row == 1, sy, sz))
    mask = jnp.zeros((1, LANES), jnp.float32)
    for t in range(table.shape[1] // LANES):
        tile = table[:, t * LANES : (t + 1) * LANES]
        low, high = jnp.min(tile, axis=1, keepdims=True), jnp.max(tile, axis=1, keepdims=True)
        gap = jnp.maximum(jnp.maximum(low + shift - 1.0, -(high + shift)), 0.0)
        apart = jnp.sum(jnp.where(row < 3, gap * gap, 0.0), axis=0, keepdims=True)
        mask = mask + jnp.where(apart < REACH2, float(1 << t), 0.0)
    return mask


def order_active(table, place, index_row, act_ref, arow_ref, rank_ref, mask_ref, e):
    width = table.shape[1]
    picked = index_row.shape[1]
    eye = lax.broadcasted_iota(jnp.int32, (picked, picked), 0) == lax.broadcasted_iota(
        jnp.int32, (picked, picked), 1
    )
    index_f = index_row.astype(jnp.float32)
    index_col = jnp.sum(jnp.where(eye, index_f, 0.0), axis=1, keepdims=True)
    lane = lax.broadcasted_iota(jnp.int32, (picked, width), 1).astype(jnp.float32)
    spot_col = jnp.sum(jnp.where(lane == index_col, place, 0.0), axis=1, keepdims=True)
    sel = jnp.where(lane == spot_col, 1.0, 0.0)
    index_f = jnp.sum(jnp.where(eye, spot_col, 0.0), axis=0, keepdims=True)
    sel16 = sel.astype(jnp.bfloat16)
    three = split_three(table)
    parts = lax.dot_general(three, sel16, CONTRACT, preferred_element_type=jnp.float32)
    rows = parts[:8] + parts[8:16] + parts[16:]
    parts = lax.dot_general(sel16, three, CONTRACT, preferred_element_type=jnp.float32)
    cols = parts[:, :8] + parts[:, 8:16] + parts[:, 16:]
    ii = lax.broadcasted_iota(jnp.int32, (picked, picked), 0)
    jj = lax.broadcasted_iota(jnp.int32, (picked, picked), 1)
    same = jj >= 0
    place_c = jnp.zeros((picked, 1), jnp.float32)
    place_r = jnp.zeros((1, picked), jnp.float32)
    size = picked
    for axis in range(3):
        col, row = cols[:, axis : axis + 1], rows[axis : axis + 1, :]
        in_col = jnp.logical_and(same, below(row, col, jj < ii))
        in_row = jnp.logical_and(same, below(col, row, ii < jj))
        rank_c = jnp.sum(jnp.where(in_col, 1.0, 0.0), axis=1, keepdims=True)
        rank_r = jnp.sum(jnp.where(in_row, 1.0, 0.0), axis=0, keepdims=True)
        if axis == 2:
            place_c = place_c + rank_c
            place_r = place_r + rank_r
            break
        size //= 2
        half_c = jnp.where(rank_c >= size, float(size), 0.0)
        half_r = jnp.where(rank_r >= size, float(size), 0.0)
        place_c = place_c + half_c
        place_r = place_r + half_r
        same = jnp.logical_and(same, half_c == half_r)
    perm = (ii.astype(jnp.float32) == place_r).astype(jnp.float32)
    ordered = lax.dot_general(
        perm, cols, (((1,), (0,)), ((), ())), precision=HIGHEST, preferred_element_type=jnp.float32
    )
    act_ref[e] = ordered
    arow_ref[e] = jnp.sum(perm * index_f, axis=1, keepdims=True).astype(jnp.int32)
    rank_ref[e] = place_r
    boxes = ordered.reshape(picked // 8, 8, ordered.shape[1])
    low, high = jnp.min(boxes, axis=1), jnp.max(boxes, axis=1)
    shifts = code_shifts(picked // 8)
    apart = jnp.zeros((picked // 8, LANES), jnp.float32)
    for axis, shift in enumerate(shifts):
        gap = jnp.maximum(low[:, axis : axis + 1] - (shift + 1.0), shift - high[:, axis : axis + 1])
        gap = jnp.maximum(gap, 0.0)
        apart = apart + gap * gap
    bit = jnp.left_shift(1, lax.broadcasted_iota(jnp.int32, (picked // 8, LANES), 0)).astype(jnp.float32)
    mask_ref[e] = jnp.sum(jnp.where(apart < REACH2, bit, 0.0), axis=0, keepdims=True).astype(jnp.int32)


def first_kernel(
    n_cells, n_grp, pos_ref, vel_ref, smooth_ref, mass_ref, entropy_ref, old_ref, index_ref, pairs_ref,
    all_ref, rows_ref, act_ref, arow_ref, rank_ref, mask_ref, own_ref,
    table, listing, sends, recvs, local_sem,
):
    cells, width = smooth_ref.shape
    mate, mine, others = routes(n_cells, n_grp)
    greet(mate, others)
    place = tile_order(pos_ref[0], pos_ref[1])
    pairs = pairs_ref[...].astype(jnp.float32)
    fields = pairs.shape[1]
    eye = (
        lax.broadcasted_iota(jnp.int32, (8, fields), 0) == lax.broadcasted_iota(jnp.int32, (8, fields), 1)
    ).astype(jnp.float32)
    listing[...] = jnp.zeros_like(listing)
    listing[0:8, 0 : pairs.shape[0]] = lax.dot_general(
        eye, pairs, CONTRACT, precision=HIGHEST, preferred_element_type=jnp.float32
    )
    for e in range(cells):
        here = slice(e, e + 1)
        rows = jnp.concatenate(
            [pos_ref[d, here] for d in range(3)]
            + [vel_ref[d, here] for d in range(3)]
            + [smooth_ref[here], mass_ref[here], entropy_ref[here], old_ref[here]]
            + [jnp.zeros((6, width), jnp.float32)],
            axis=0,
        )
        moved = permuted(rows, place[here])
        table[e] = moved[:8]
        table[cells, here] = moved[8:9]
        own_ref[0, here] = moved[8:9]
        own_ref[1, here] = moved[9:10]
        listing[8 + e : 9 + e, 0:LANES] = tile_mask(moved[:8])
    pieces = ((listing, rows_ref), (table, all_ref))
    first, rest, count = spread(mate, mine, others, pieces, sends, recvs, local_sem)
    for e in range(cells):
        order_active(
            table[e], place[e : e + 1], index_ref[e : e + 1], act_ref, arow_ref, rank_ref, mask_ref, e
        )
    forward(mate, others, pieces, first, rest, count, sends, recvs)


def second_kernel(n_cells, n_grp, mine_ref, all_ref, sends, recvs, local_sem):
    mate, mine, others = routes(n_cells, n_grp)
    greet(mate, others)
    pieces = ((mine_ref, all_ref),)
    first, rest, count = spread(mate, mine, others, pieces, sends, recvs, local_sem)
    forward(mate, others, pieces, first, rest, count, sends, recvs)


def unit_shift(word):
    return [((word >> bits) & 3).astype(jnp.float32) - 1.0 for bits in (18, 20, 22)]


def unit_place(word):
    return word & 63, (word >> 6) & 127, pl.ds(pl.multiple_of(((word >> 24) & 3) * LANES, LANES), LANES)


def density_kernel(
    words_ref, mask_ref, tiles_ref, table_ref, act_ref, arow_ref, rank_ref, own_ref,
    rho_out, rho_col, press_col, state_out, units_ref, count_ref,
    entries, spans, wide, acc,
):
    cells, picked, _ = act_ref.shape
    width = table_ref.shape[2]
    groups = picked // 8
    total = words_ref.shape[0]

    def keep(step, found):
        for k in range(8):
            word = words_ref[step * 8 + k]
            entries[found] = word
            found = found + (word >> 21)
        return found

    found = lax.fori_loop(0, total // 8, keep, jnp.int32(0))

    def unroll(step, count):
        word = entries[step]
        bits = tiles_ref[((word >> 3) & 127) * LANES + ((word >> 10) & 31)]
        base = word & 0x1FFFFF
        for t in range(width // LANES):
            spans[count] = base + (t << 21)
            count = count + ((bits >> t) & 1)
        return count

    spanned = lax.fori_loop(0, found, unroll, jnp.int32(0))

    def unfold(step, count):
        word = spans[step]
        bits = mask_ref[(word & 7) * LANES + ((word >> 10) & 31)]
        base = word << 3
        for g in range(groups):
            units_ref[count] = base + g
            count = count + ((bits >> g) & 1)
        return count

    count = lax.fori_loop(0, spanned, unfold, jnp.int32(0))
    for k in range(BATCH):
        units_ref[count + k] = jnp.int32(FAR_WORD)
    count_ref[0] = count

    for e in range(cells):
        data = act_ref[e]
        for f, col in enumerate((data[:, 0:1], data[:, 1:2], data[:, 2:3], 1.0 / (data[:, 6:7] * data[:, 6:7]))):
            wide[f, e * groups : (e + 1) * groups] = jnp.broadcast_to(col, (picked, LANES)).reshape(
                groups, 8, LANES
            )
    acc[...] = jnp.zeros_like(acc)

    def batch(step, carry):
        results = []
        for k in range(BATCH):
            word = units_ref[step * BATCH + k]
            ig, far, at = unit_place(word)
            ox, oy, oz = unit_shift(word)
            block = far + (far >> 3)
            dx = (wide[0, ig] - ox) - table_ref[block, 0:1, at]
            dy = (wide[1, ig] - oy) - table_ref[block, 1:2, at]
            dz = (wide[2, ig] - oz) - table_ref[block, 2:3, at]
            q2 = (dx * dx + dy * dy + dz * dz) * wide[3, ig]
            q = q2 * lax.rsqrt(jnp.maximum(q2, 1e-30))
            u = 1.0 - q
            w = jnp.maximum(u + 1.0, 0.0)
            u = jnp.maximum(u, 0.0)
            results.append((ig, table_ref[block, 7:8, at] * (0.25 * (w * w * w) - u * u * u)))
        for ig, part in results:
            acc[ig] += part
        return carry

    lax.fori_loop(0, (count + BATCH - 1) // BATCH, batch, 0)

    ii = lax.broadcasted_iota(jnp.int32, (picked, picked), 0).astype(jnp.float32)
    lane = lax.broadcasted_iota(jnp.int32, (picked, width), 1)
    for e in range(cells):
        h = act_ref[e][:, 6:7]
        col = jnp.sum(acc[e * groups : (e + 1) * groups].reshape(picked, LANES), axis=1, keepdims=True)
        col = col / (math.pi * h * h * h)
        rho_out[e : e + 1, :] = jnp.sum(jnp.where(ii == rank_ref[e], col, 0.0), axis=0, keepdims=True)
        hit = lane == arow_ref[e]
        entropy = own_ref[0, e : e + 1, :]
        placed = jnp.sum(jnp.where(hit, col, 0.0), axis=0, keepdims=True)
        any_hit = jnp.sum(jnp.where(hit, 1.0, 0.0), axis=0, keepdims=True)
        rho = jnp.where(any_hit > 0.0, placed, own_ref[1, e : e + 1, :])
        own_entropy = jnp.sum(jnp.where(hit, entropy, 0.0), axis=1, keepdims=True)
        state_out[e : e + 1, :] = rho
        rho_col[e] = col
        press_col[e] = own_entropy * jnp.exp(jnp.log(col) * (-1.0 / 3.0))


def inverse(x):
    y = pl.reciprocal(x, approx=True)
    return y * (2.0 - x * y)


def force_kernel(
    units_ref, count_ref, table_ref, state_ref, act_ref, rho_col, press_col, rank_ref,
    acc_out, wide, acc, state,
):
    cells, picked, _ = act_ref.shape
    width = table_ref.shape[2]
    groups = picked // 8
    for e in range(cells):
        data = act_ref[e]
        rho, press = rho_col[e], press_col[e]
        sound = 0.5 * jnp.sqrt(GAMMA * press * rho)
        fields = [data[:, f : f + 1] for f in range(6)] + [0.5 * data[:, 6:7], press, rho, sound]
        for f, col in enumerate(fields):
            wide[f, e * groups : (e + 1) * groups] = jnp.broadcast_to(col, (picked, LANES)).reshape(
                groups, 8, LANES
            )
    acc[...] = jnp.zeros_like(acc)

    for slot in range(state_ref.shape[0]):
        rho = state_ref[slot]
        press = table_ref[slot * (cells + 1) + cells] * jnp.exp(jnp.log(rho) * (-1.0 / 3.0))
        sound = 0.5 * jnp.sqrt(GAMMA * press * rho)
        for e in range(cells):
            for f, value in enumerate((rho, press, sound)):
                state[slot * cells + e, f : f + 1] = value[e : e + 1]

    def batch(step, carry):
        results = []
        for k in range(BATCH):
            word = units_ref[step * BATCH + k]
            ig, far, at = unit_place(word)
            ox, oy, oz = unit_shift(word)
            block = far + (far >> 3)
            dx = (wide[0, ig] - ox) - table_ref[block, 0:1, at]
            dy = (wide[1, ig] - oy) - table_ref[block, 1:2, at]
            dz = (wide[2, ig] - oz) - table_ref[block, 2:3, at]
            du = wide[3, ig] - table_ref[block, 3:4, at]
            dv = wide[4, ig] - table_ref[block, 4:5, at]
            dw = wide[5, ig] - table_ref[block, 5:6, at]
            r2 = dx * dx + dy * dy + dz * dz
            approach = jnp.minimum(dx * du + dy * dv + dz * dw, 0.0)
            h = wide[6, ig] + 0.5 * table_ref[block, 6:7, at]
            ih = inverse(h)
            ih2 = ih * ih
            q2 = r2 * ih2
            rq = lax.rsqrt(jnp.maximum(q2, 1e-30))
            q = q2 * rq
            w = jnp.maximum(2.0 - q, 0.0)
            slope = jnp.where(q < 1.0, 3.0 - 2.25 * q, 0.75 * (w * w) * rq)
            mu2 = 2.0 * (h * approach * inverse(r2 + 0.01 * (h * h)))
            visc = mu2 * (mu2 - (wide[9, ig] + state[far, 2:3, at])) * inverse(wide[8, ig] + state[far, 0:1, at])
            coef = (wide[7, ig] + state[far, 1:2, at] + visc) * slope
            coef = coef * (ih2 * ih2 * ih) * table_ref[block, 7:8, at]
            results.append((ig, (coef * dx, coef * dy, coef * dz)))
        for ig, parts in results:
            for axis in range(3):
                acc[axis, ig] += parts[axis]
        return carry

    lax.fori_loop(0, (count_ref[0] + BATCH - 1) // BATCH, batch, 0)
    ii = lax.broadcasted_iota(jnp.int32, (picked, picked), 0).astype(jnp.float32)
    for axis in range(3):
        for e in range(cells):
            col = jnp.sum(
                acc[axis, e * groups : (e + 1) * groups].reshape(picked, LANES), axis=1, keepdims=True
            )
            col = col * (1.0 / math.pi)
            acc_out[axis, e : e + 1, :] = jnp.sum(
                jnp.where(ii == rank_ref[e], col, 0.0), axis=0, keepdims=True
            )


def shape(dims, kind=jnp.float32):
    return jax.ShapeDtypeStruct(dims, kind)


def local(positions, velocities, smoothing, masses, entropy, density_old, active_rows, pairs):
    n_cells, n_grp = lax.axis_size("cells"), lax.axis_size("grp")
    cells, width = smoothing.shape
    picked = active_rows.shape[1]
    listed = pairs.shape[0]
    groups = picked // 8
    slots = 3 * n_grp
    padded = -(-listed // LANES) * LANES
    n_copies = slots - 1
    limit = 48 * 1024 * 1024
    far, far_rows, act, arow, rank, mask, own = pl.pallas_call(
        functools.partial(first_kernel, n_cells, n_grp),
        out_shape=(
            shape((slots, cells + 1, 8, width)),
            shape((slots, 8 + cells, padded)),
            shape((cells, picked, 8)),
            shape((cells, picked, 1), jnp.int32),
            shape((cells, 1, picked)),
            shape((cells, 1, LANES), jnp.int32),
            shape((2, cells, width)),
        ),
        in_specs=[VMEM] * 8,
        out_specs=(ANY, ANY, VMEM, VMEM, VMEM, VMEM, VMEM),
        scratch_shapes=[
            pltpu.VMEM((cells + 1, 8, width), jnp.float32),
            pltpu.VMEM((8 + cells, padded), jnp.float32),
            pltpu.SemaphoreType.DMA((2 * n_copies,)),
            pltpu.SemaphoreType.DMA((2 * n_copies,)),
            pltpu.SemaphoreType.DMA((2,)),
        ],
        compiler_params=pltpu.CompilerParams(
            collective_id=0, has_side_effects=True, vmem_limit_bytes=limit
        ),
    )(positions, velocities, smoothing, masses, entropy, density_old, active_rows, pairs)

    me_g = lax.axis_index("grp")

    def word(own, cell, code, valid):
        x, y, z = code // 9, code // 3 % 3, code % 3
        return own | (cell << 3) | (code << 10) | (x << 15) | (y << 17) | (z << 19) | (
            valid.astype(jnp.int32) << 21
        )

    home = word(
        pairs[:, 0],
        ((1 + pairs[:, 1]) * n_grp + pairs[:, 2]) * cells + pairs[:, 3],
        pairs[:, 4],
        jnp.ones((listed,), jnp.bool_),
    )
    far_rows = far_rows.astype(jnp.int32)
    tiles = far_rows[:, 8:, :LANES].reshape(-1)
    seen = far_rows[: 2 * n_grp]
    slot = lax.broadcasted_iota(jnp.int32, (2 * n_grp, listed), 0)
    seen = seen[:, :, :listed]
    ours = (seen[:, 2] == me_g) & (seen[:, 1] == jnp.where(slot < n_grp, 1, 0))
    away = word(seen[:, 3], slot * cells + seen[:, 0], seen[:, 4], ours)
    ids = jnp.arange(cells, dtype=jnp.int32)
    alone = word(ids, (n_grp + me_g) * cells + ids, jnp.full((cells,), 13, jnp.int32), ids >= 0)
    words = jnp.concatenate([home, alone, away.reshape(-1)])
    words = jnp.pad(words, (0, -words.shape[0] % 8))
    n_words = words.shape[0]
    far = far.reshape(slots * (cells + 1), 8, width)
    tiled = width // LANES

    rho_act, rho_col, press_col, state, units, count = pl.pallas_call(
        density_kernel,
        out_shape=(
            shape((cells, picked)),
            shape((cells, picked, 1)),
            shape((cells, picked, 1)),
            shape((cells, width)),
            shape((n_words * tiled * groups + 8 + BATCH,), jnp.int32),
            shape((1,), jnp.int32),
        ),
        in_specs=[SMEM] * 3 + [VMEM] * 5,
        out_specs=(VMEM, VMEM, VMEM, VMEM, SMEM, SMEM),
        scratch_shapes=[
            pltpu.SMEM((n_words + 8,), jnp.int32),
            pltpu.SMEM((n_words * tiled + 8,), jnp.int32),
            pltpu.VMEM((4, cells * groups, 8, LANES), jnp.float32),
            pltpu.VMEM((cells * groups, 8, LANES), jnp.float32),
        ],
        compiler_params=pltpu.CompilerParams(vmem_limit_bytes=limit),
    )(words, mask.reshape(-1), tiles, far, act, arow, rank, own)

    far_state = pl.pallas_call(
        functools.partial(second_kernel, n_cells, n_grp),
        out_shape=shape((slots, cells, width)),
        in_specs=[VMEM],
        out_specs=ANY,
        scratch_shapes=[
            pltpu.SemaphoreType.DMA((n_copies,)),
            pltpu.SemaphoreType.DMA((n_copies,)),
            pltpu.SemaphoreType.DMA((1,)),
        ],
        compiler_params=pltpu.CompilerParams(collective_id=1, has_side_effects=True),
    )(state)

    acceleration = pl.pallas_call(
        force_kernel,
        out_shape=shape((3, cells, picked)),
        in_specs=[SMEM, SMEM] + [VMEM] * 6,
        out_specs=VMEM,
        scratch_shapes=[
            pltpu.VMEM((10, cells * groups, 8, LANES), jnp.float32),
            pltpu.VMEM((3, cells * groups, 8, LANES), jnp.float32),
            pltpu.VMEM((slots * cells, 8, width), jnp.float32),
        ],
        compiler_params=pltpu.CompilerParams(vmem_limit_bytes=limit),
    )(units, count, far, far_state, act, rho_col, press_col, rank)
    return rho_act, acceleration


def solution(mesh):
    split = ("cells", "grp")
    return jax.shard_map(
        local,
        mesh=mesh,
        in_specs=(
            P(None, split, None),
            P(None, split, None),
            P(split, None),
            P(split, None),
            P(split, None),
            P(split, None),
            P(split, None),
            P(split, None),
        ),
        out_specs=(P(split, None), P(None, split, None)),
        check_vma=False,
    )
```

```python
import functools
import math

import jax
import jax.numpy as jnp
from jax import lax
from jax.experimental import pallas as pl
from jax.experimental.pallas import tpu as pltpu
from jax.sharding import PartitionSpec as P

GAMMA = 5.0 / 3.0
HIGHEST = lax.Precision.HIGHEST
REACH2 = 0.1601
LANES = 128
BATCH = 8
FAR_WORD = (3 << 18) | (3 << 20) | (3 << 22)
MESH = pl.DeviceIdType.MESH
VMEM = pl.BlockSpec(memory_space=pltpu.VMEM)
SMEM = pl.BlockSpec(memory_space=pltpu.SMEM)
ANY = pl.BlockSpec(memory_space=pl.ANY)
CONTRACT = (((1,), (1,)), ((), ()))


def routes(n_cells, n_grp):
    me_c, me_g = lax.axis_index("cells"), lax.axis_index("grp")
    out = []
    for step in (0, 1, -1):
        for turn in range(0, n_grp, 2):
            if step == 0 and turn == 0:
                continue
            there = (lax.rem(me_c + step + n_cells, n_cells), lax.rem(me_g + turn, n_grp))
            base = (1 - step) * n_grp
            out.append((there, base + me_g, base + lax.rem(me_g - turn + n_grp, n_grp)))
    mate = (me_c, me_g + 1 - 2 * lax.rem(me_g, 2))
    return mate, n_grp + me_g, out


def greet(mate, others):
    barrier = pltpu.get_barrier_semaphore()
    for there in [mate] + [other[0] for other in others]:
        pl.semaphore_signal(barrier, inc=1, device_id=there, device_id_type=MESH)
    pl.semaphore_wait(barrier, len(others) + 1)


def remote(src, dst, sends, recvs, index, there):
    copy = pltpu.make_async_remote_copy(
        src_ref=src,
        dst_ref=dst,
        send_sem=sends.at[index],
        recv_sem=recvs.at[index],
        device_id=there,
        device_id_type=MESH,
    )
    copy.start()
    return copy


def spread(mate, mine, others, pieces, sends, recvs, local_sem):
    first, rest = [], []
    count = 0
    for there, slot, _ in others:
        for src, dst in pieces:
            first.append(remote(src, dst.at[slot], sends, recvs, count, there))
            count += 1
    for index, (src, dst) in enumerate(pieces):
        rest.append(remote(src, dst.at[mine], sends, recvs, count, mate))
        count += 1
        copy = pltpu.make_async_copy(src, dst.at[mine], local_sem.at[index])
        copy.start()
        rest.append(copy)
    return first, rest, count


def forward(mate, others, pieces, first, rest, count, sends, recvs):
    at = 0
    for _, _, slot in others:
        for _, dst in pieces:
            first[at].wait_recv()
            rest.append(remote(dst.at[slot], dst.at[slot], sends, recvs, count, mate))
            at += 1
            count += 1
    for copy in first:
        copy.wait_send()
    for copy in rest:
        copy.wait()


def below(row, col, first):
    return jnp.logical_or(row < col, jnp.logical_and(row == col, first))


def code_shifts(rows):
    code = lax.broadcasted_iota(jnp.int32, (rows, LANES), 1).astype(jnp.float32)
    top = jnp.where(code >= 9.0, 1.0, 0.0) + jnp.where(code >= 18.0, 1.0, 0.0)
    rest = code - 9.0 * top
    mid = jnp.where(rest >= 3.0, 1.0, 0.0) + jnp.where(rest >= 6.0, 1.0, 0.0)
    return top - 1.0, mid - 1.0, rest - 3.0 * mid - 1.0


def rank_rows(keys):
    cells, width = keys.shape
    turned = jnp.transpose(keys)
    out = []
    for e in range(cells):
        row = jnp.broadcast_to(keys[e : e + 1, :], (8, width))
        total = jnp.zeros((8, width), jnp.float32)
        for r in range(0, width, 8):
            total = total + jnp.where(turned[r : r + 8, e : e + 1] < row, 1.0, 0.0)
        out.append(jnp.sum(total, axis=0, keepdims=True))
    return jnp.concatenate(out, axis=0)


def tile_order(xs, ys):
    lane = lax.broadcasted_iota(jnp.int32, xs.shape, 1).astype(jnp.float32)
    width = xs.shape[1]
    steps = 8192.0
    half = rank_rows(jnp.floor(xs * steps) * width + lane) >= width // 2
    key = jnp.floor(ys * steps) * width + lane
    return rank_rows(key + jnp.where(half, (steps + 1.0) * width, 0.0))


def split_three(x):
    top = x.astype(jnp.bfloat16)
    rest = x - top.astype(jnp.float32)
    mid = rest.astype(jnp.bfloat16)
    low = (rest - mid.astype(jnp.float32)).astype(jnp.bfloat16)
    return jnp.concatenate([top, mid, low], axis=0)


def permuted(rows, place):
    count, width = rows.shape
    spot = lax.broadcasted_iota(jnp.int32, (width, width), 0).astype(jnp.float32)
    moved = jnp.where(spot == place, 1.0, 0.0).astype(jnp.bfloat16)
    parts = lax.dot_general(split_three(rows), moved, CONTRACT, preferred_element_type=jnp.float32)
    return parts[:count] + parts[count : 2 * count] + parts[2 * count :]


def tile_mask(table):
    row = lax.broadcasted_iota(jnp.int32, (8, LANES), 0)
    sx, sy, sz = code_shifts(8)
    shift = jnp.where(row == 0, sx, jnp.where(row == 1, sy, sz))
    code = lax.broadcasted_iota(jnp.int32, (1, LANES), 1)
    mask = jnp.zeros((1, LANES), jnp.float32)
    scale = jnp.ones((1, LANES), jnp.float32)
    for t in range(table.shape[1] // LANES):
        tile = table[:, t * LANES : (t + 1) * LANES]
        low, high = jnp.min(tile, axis=1, keepdims=True), jnp.max(tile, axis=1, keepdims=True)
        gap = jnp.maximum(jnp.maximum(low + shift - 1.0, -(high + shift)), 0.0)
        apart = jnp.sum(jnp.where(row < 3, gap * gap, 0.0), axis=0, keepdims=True)
        near = jnp.logical_and(apart < REACH2, code < 27)
        mask = mask + jnp.where(near, t * scale + 256.0, 0.0)
        scale = jnp.where(near, 4.0 * scale, scale)
    return mask


def order_active(table, place, index_row, act_ref, arow_ref, rank_ref, mask_ref, e):
    width = table.shape[1]
    picked = index_row.shape[1]
    eye = lax.broadcasted_iota(jnp.int32, (picked, picked), 0) == lax.broadcasted_iota(
        jnp.int32, (picked, picked), 1
    )
    index_f = index_row.astype(jnp.float32)
    index_col = jnp.sum(jnp.where(eye, index_f, 0.0), axis=1, keepdims=True)
    lane = lax.broadcasted_iota(jnp.int32, (picked, width), 1).astype(jnp.float32)
    spot_col = jnp.sum(jnp.where(lane == index_col, place, 0.0), axis=1, keepdims=True)
    sel = jnp.where(lane == spot_col, 1.0, 0.0)
    index_f = jnp.sum(jnp.where(eye, spot_col, 0.0), axis=0, keepdims=True)
    sel16 = sel.astype(jnp.bfloat16)
    three = split_three(table)
    parts = lax.dot_general(three, sel16, CONTRACT, preferred_element_type=jnp.float32)
    rows = parts[:8] + parts[8:16] + parts[16:]
    parts = lax.dot_general(sel16, three, CONTRACT, preferred_element_type=jnp.float32)
    cols = parts[:, :8] + parts[:, 8:16] + parts[:, 16:]
    ii = lax.broadcasted_iota(jnp.int32, (picked, picked), 0)
    jj = lax.broadcasted_iota(jnp.int32, (picked, picked), 1)
    same = jj >= 0
    place_c = jnp.zeros((picked, 1), jnp.float32)
    place_r = jnp.zeros((1, picked), jnp.float32)
    size = picked
    for axis in range(3):
        col, row = cols[:, axis : axis + 1], rows[axis : axis + 1, :]
        in_col = jnp.logical_and(same, below(row, col, jj < ii))
        in_row = jnp.logical_and(same, below(col, row, ii < jj))
        rank_c = jnp.sum(jnp.where(in_col, 1.0, 0.0), axis=1, keepdims=True)
        rank_r = jnp.sum(jnp.where(in_row, 1.0, 0.0), axis=0, keepdims=True)
        if axis == 2:
            place_c = place_c + rank_c
            place_r = place_r + rank_r
            break
        size //= 2
        half_c = jnp.where(rank_c >= size, float(size), 0.0)
        half_r = jnp.where(rank_r >= size, float(size), 0.0)
        place_c = place_c + half_c
        place_r = place_r + half_r
        same = jnp.logical_and(same, half_c == half_r)
    perm = (ii.astype(jnp.float32) == place_r).astype(jnp.float32)
    ordered = lax.dot_general(
        perm, cols, (((1,), (0,)), ((), ())), precision=HIGHEST, preferred_element_type=jnp.float32
    )
    act_ref[e] = ordered
    arow_ref[e] = jnp.sum(perm * index_f, axis=1, keepdims=True).astype(jnp.int32)
    rank_ref[e] = place_r
    boxes = ordered.reshape(picked // 8, 8, ordered.shape[1])
    low, high = jnp.min(boxes, axis=1), jnp.max(boxes, axis=1)
    shifts = code_shifts(picked // 8)
    apart = jnp.zeros((picked // 8, LANES), jnp.float32)
    for axis, shift in enumerate(shifts):
        gap = jnp.maximum(low[:, axis : axis + 1] - (shift + 1.0), shift - high[:, axis : axis + 1])
        gap = jnp.maximum(gap, 0.0)
        apart = apart + gap * gap
    near = jnp.where(apart < REACH2, 1, 0)
    code = lax.broadcasted_iota(jnp.int32, (1, LANES), 1)
    mask = jnp.zeros((1, LANES), jnp.int32)
    found = jnp.zeros((1, LANES), jnp.int32)
    for g in range(picked // 8):
        here = near[g : g + 1]
        mask = mask + here * jnp.left_shift(jnp.full((1, LANES), g, jnp.int32), 3 * found)
        found = found + here
    mask_ref[e] = jnp.where(code < 27, mask + jnp.left_shift(found, 24), 0)


def first_kernel(
    n_cells, n_grp, pos_in, vel_in, smooth_in, mass_in, entropy_in, old_in, index_in, pairs_in,
    all_ref, rows_ref, act_ref, arow_ref, rank_ref, mask_ref, own_ref,
    pos_ref, vel_ref, smooth_ref, mass_ref, entropy_ref, old_ref, index_ref, pairs_ref,
    table, listing, sends, recvs, local_sem, load_sem,
):
    cells, width = smooth_ref.shape
    mate, mine, others = routes(n_cells, n_grp)
    loads = []
    for src, dst in (
        (pos_in, pos_ref),
        (vel_in, vel_ref),
        (smooth_in, smooth_ref),
        (mass_in, mass_ref),
        (entropy_in, entropy_ref),
        (old_in, old_ref),
        (index_in, index_ref),
        (pairs_in, pairs_ref),
    ):
        load = pltpu.make_async_copy(src, dst, load_sem.at[len(loads)])
        load.start()
        loads.append(load)
    greet(mate, others)
    for load in loads:
        load.wait()
    place = tile_order(pos_ref[0], pos_ref[1])
    listing[...] = jnp.zeros_like(listing)
    listing[0 : pairs_ref.shape[0], 0 : pairs_ref.shape[1]] = pairs_ref[...].astype(jnp.float32)
    for e in range(cells):
        here = slice(e, e + 1)
        rows = jnp.concatenate(
            [pos_ref[d, here] for d in range(3)]
            + [vel_ref[d, here] for d in range(3)]
            + [smooth_ref[here], mass_ref[here], entropy_ref[here], old_ref[here]]
            + [jnp.zeros((6, width), jnp.float32)],
            axis=0,
        )
        moved = permuted(rows, place[here])
        table[e] = moved[:8]
        table[cells, here] = moved[8:9]
        own_ref[0, here] = moved[8:9]
        own_ref[1, here] = moved[9:10]
        listing[8 + e : 9 + e, 0:LANES] = tile_mask(moved[:8])
    pieces = ((listing, rows_ref), (table, all_ref))
    first, rest, count = spread(mate, mine, others, pieces, sends, recvs, local_sem)
    for e in range(cells):
        order_active(
            table[e], place[e : e + 1], index_ref[e : e + 1], act_ref, arow_ref, rank_ref, mask_ref, e
        )
    forward(mate, others, pieces, first, rest, count, sends, recvs)


def second_kernel(n_cells, n_grp, mine_ref, all_ref, sends, recvs, local_sem):
    mate, mine, others = routes(n_cells, n_grp)
    greet(mate, others)
    pieces = ((mine_ref, all_ref),)
    first, rest, count = spread(mate, mine, others, pieces, sends, recvs, local_sem)
    forward(mate, others, pieces, first, rest, count, sends, recvs)


def unit_shift(word):
    return [((word >> bits) & 3).astype(jnp.float32) - 1.0 for bits in (18, 20, 22)]


def unit_place(word):
    return word & 63, (word >> 6) & 127, pl.ds(pl.multiple_of(((word >> 24) & 3) * LANES, LANES), LANES)


def density_kernel(
    words_ref, mask_ref, tiles_ref, table_ref, act_ref, arow_ref, rank_ref, own_ref,
    rho_out, rho_col, press_col, state_out, units_ref, count_ref,
    entries, spans, wide, acc,
):
    cells, picked, _ = act_ref.shape
    width = table_ref.shape[2]
    groups = picked // 8
    total = words_ref.shape[0]

    def keep(step, found):
        held = [words_ref[step * 8 + k] for k in range(8)]
        for word in held:
            entries[found] = word
            found = found + (word >> 21)
        return found

    found = lax.fori_loop(0, total // 8, keep, jnp.int32(0))
    for k in range(4):
        entries[found + k] = jnp.int32(31 << 10)

    def unroll(step, count):
        held = [entries[step * 4 + k] for k in range(4)]
        lists = [tiles_ref[((word >> 3) & 127) * LANES + ((word >> 10) & 31)] for word in held]
        for word, listed in zip(held, lists):
            base = word & 0x1FFFFF
            for t in range(width // LANES):
                spans[count + t] = base + (((listed >> (2 * t)) & 3) << 21)
            count = count + (listed >> 8)
        return count

    spanned = lax.fori_loop(0, (found + 3) // 4, unroll, jnp.int32(0))
    for k in range(4):
        spans[spanned + k] = jnp.int32(31 << 10)

    def unfold(step, count):
        held = [spans[step * 4 + k] for k in range(4)]
        lists = [mask_ref[(word & 7) * LANES + ((word >> 10) & 31)] for word in held]
        for word, listed in zip(held, lists):
            base = word << 3
            for g in range(groups):
                units_ref[count + g] = base + ((listed >> (3 * g)) & 7)
            count = count + (listed >> 24)
        return count

    count = lax.fori_loop(0, (spanned + 3) // 4, unfold, jnp.int32(0))
    for k in range(BATCH):
        units_ref[count + k] = jnp.int32(FAR_WORD)
    count_ref[0] = count

    for e in range(cells):
        data = act_ref[e]
        for f, col in enumerate((data[:, 0:1], data[:, 1:2], data[:, 2:3], 1.0 / (data[:, 6:7] * data[:, 6:7]))):
            wide[f, e * groups : (e + 1) * groups] = jnp.broadcast_to(col, (picked, LANES)).reshape(
                groups, 8, LANES
            )
    acc[...] = jnp.zeros_like(acc)

    def batch(step, carry):
        results = []
        for k in range(BATCH):
            word = units_ref[step * BATCH + k]
            ig, far, at = unit_place(word)
            ox, oy, oz = unit_shift(word)
            block = far + (far >> 3)
            dx = (wide[0, ig] - ox) - table_ref[block, 0:1, at]
            dy = (wide[1, ig] - oy) - table_ref[block, 1:2, at]
            dz = (wide[2, ig] - oz) - table_ref[block, 2:3, at]
            q2 = (dx * dx + dy * dy + dz * dz) * wide[3, ig]
            q = q2 * lax.rsqrt(jnp.maximum(q2, 1e-30))
            u = 1.0 - q
            w = jnp.maximum(u + 1.0, 0.0)
            u = jnp.maximum(u, 0.0)
            results.append((ig, table_ref[block, 7:8, at] * (0.25 * (w * w * w) - u * u * u)))
        for ig, part in results:
            acc[ig] += part
        return carry

    lax.fori_loop(0, (count + BATCH - 1) // BATCH, batch, 0)

    ii = lax.broadcasted_iota(jnp.int32, (picked, picked), 0).astype(jnp.float32)
    lane = lax.broadcasted_iota(jnp.int32, (picked, width), 1)
    for e in range(cells):
        h = act_ref[e][:, 6:7]
        col = jnp.sum(acc[e * groups : (e + 1) * groups].reshape(picked, LANES), axis=1, keepdims=True)
        col = col / (math.pi * h * h * h)
        rho_out[e : e + 1, :] = jnp.sum(jnp.where(ii == rank_ref[e], col, 0.0), axis=0, keepdims=True)
        hit = lane == arow_ref[e]
        entropy = own_ref[0, e : e + 1, :]
        placed = jnp.sum(jnp.where(hit, col, 0.0), axis=0, keepdims=True)
        any_hit = jnp.sum(jnp.where(hit, 1.0, 0.0), axis=0, keepdims=True)
        rho = jnp.where(any_hit > 0.0, placed, own_ref[1, e : e + 1, :])
        own_entropy = jnp.sum(jnp.where(hit, entropy, 0.0), axis=1, keepdims=True)
        state_out[e : e + 1, :] = rho
        rho_col[e] = col
        press_col[e] = own_entropy * jnp.exp(jnp.log(col) * (-1.0 / 3.0))


def inverse(x):
    return pl.reciprocal(x, approx=True)


def force_kernel(
    units_ref, count_ref, table_ref, state_ref, act_ref, rho_col, press_col, rank_ref,
    acc_out, wide, acc, state,
):
    cells, picked, _ = act_ref.shape
    width = table_ref.shape[2]
    groups = picked // 8
    for e in range(cells):
        data = act_ref[e]
        rho, press = rho_col[e], press_col[e]
        sound = 0.5 * jnp.sqrt(GAMMA * press * rho)
        fields = [data[:, f : f + 1] for f in range(6)] + [0.5 * data[:, 6:7], press, rho, sound]
        for f, col in enumerate(fields):
            wide[f, e * groups : (e + 1) * groups] = jnp.broadcast_to(col, (picked, LANES)).reshape(
                groups, 8, LANES
            )
    acc[...] = jnp.zeros_like(acc)

    for slot in range(state_ref.shape[0]):
        rho = state_ref[slot]
        press = table_ref[slot * (cells + 1) + cells] * jnp.exp(jnp.log(rho) * (-1.0 / 3.0))
        sound = 0.5 * jnp.sqrt(GAMMA * press * rho)
        for e in range(cells):
            for f, value in enumerate((rho, press, sound)):
                state[slot * cells + e, f : f + 1] = value[e : e + 1]

    def batch(step, carry):
        results = []
        for k in range(BATCH):
            word = units_ref[step * BATCH + k]
            ig, far, at = unit_place(word)
            ox, oy, oz = unit_shift(word)
            block = far + (far >> 3)
            dx = (wide[0, ig] - ox) - table_ref[block, 0:1, at]
            dy = (wide[1, ig] - oy) - table_ref[block, 1:2, at]
            dz = (wide[2, ig] - oz) - table_ref[block, 2:3, at]
            du = wide[3, ig] - table_ref[block, 3:4, at]
            dv = wide[4, ig] - table_ref[block, 4:5, at]
            dw = wide[5, ig] - table_ref[block, 5:6, at]
            r2 = dx * dx + dy * dy + dz * dz
            approach = jnp.minimum(dx * du + dy * dv + dz * dw, 0.0)
            h = wide[6, ig] + 0.5 * table_ref[block, 6:7, at]
            ih = inverse(h)
            ih2 = ih * ih
            q2 = r2 * ih2
            rq = lax.rsqrt(jnp.maximum(q2, 1e-30))
            q = q2 * rq
            w = jnp.maximum(2.0 - q, 0.0)
            slope = jnp.where(q < 1.0, 3.0 - 2.25 * q, 0.75 * (w * w) * rq)
            mu2 = 2.0 * (h * approach * inverse(r2 + 0.01 * (h * h)))
            visc = mu2 * (mu2 - (wide[9, ig] + state[far, 2:3, at])) * inverse(wide[8, ig] + state[far, 0:1, at])
            coef = (wide[7, ig] + state[far, 1:2, at] + visc) * slope
            coef = coef * (ih2 * ih2 * ih) * table_ref[block, 7:8, at]
            results.append((ig, (coef * dx, coef * dy, coef * dz)))
        for ig, parts in results:
            for axis in range(3):
                acc[axis, ig] += parts[axis]
        return carry

    lax.fori_loop(0, (count_ref[0] + BATCH - 1) // BATCH, batch, 0)
    ii = lax.broadcasted_iota(jnp.int32, (picked, picked), 0).astype(jnp.float32)
    for axis in range(3):
        for e in range(cells):
            col = jnp.sum(
                acc[axis, e * groups : (e + 1) * groups].reshape(picked, LANES), axis=1, keepdims=True
            )
            col = col * (1.0 / math.pi)
            acc_out[axis, e : e + 1, :] = jnp.sum(
                jnp.where(ii == rank_ref[e], col, 0.0), axis=0, keepdims=True
            )


def shape(dims, kind=jnp.float32):
    return jax.ShapeDtypeStruct(dims, kind)


def local(positions, velocities, smoothing, masses, entropy, density_old, active_rows, pairs):
    n_cells, n_grp = lax.axis_size("cells"), lax.axis_size("grp")
    cells, width = smoothing.shape
    picked = active_rows.shape[1]
    listed = pairs.shape[0]
    groups = picked // 8
    slots = 3 * n_grp
    padded = -(-listed // LANES) * LANES
    n_copies = slots - 1
    limit = 48 * 1024 * 1024
    far, far_rows, act, arow, rank, mask, own = pl.pallas_call(
        functools.partial(first_kernel, n_cells, n_grp),
        out_shape=(
            shape((slots, cells + 1, 8, width)),
            shape((slots, 8 + cells, padded)),
            shape((cells, picked, 8)),
            shape((cells, picked, 1), jnp.int32),
            shape((cells, 1, picked)),
            shape((cells, 1, LANES), jnp.int32),
            shape((2, cells, width)),
        ),
        in_specs=[ANY] * 8,
        out_specs=(ANY, ANY, VMEM, VMEM, VMEM, VMEM, VMEM),
        scratch_shapes=[
            pltpu.VMEM((3, cells, width), jnp.float32),
            pltpu.VMEM((3, cells, width), jnp.float32),
            pltpu.VMEM((cells, width), jnp.float32),
            pltpu.VMEM((cells, width), jnp.float32),
            pltpu.VMEM((cells, width), jnp.float32),
            pltpu.VMEM((cells, width), jnp.float32),
            pltpu.VMEM((cells, picked), jnp.int32),
            pltpu.VMEM((pairs.shape[1], listed), jnp.int32),
            pltpu.VMEM((cells + 1, 8, width), jnp.float32),
            pltpu.VMEM((8 + cells, padded), jnp.float32),
            pltpu.SemaphoreType.DMA((2 * n_copies,)),
            pltpu.SemaphoreType.DMA((2 * n_copies,)),
            pltpu.SemaphoreType.DMA((2,)),
            pltpu.SemaphoreType.DMA((8,)),
        ],
        compiler_params=pltpu.CompilerParams(
            collective_id=0, has_side_effects=True, vmem_limit_bytes=limit
        ),
    )(positions, velocities, smoothing, masses, entropy, density_old, active_rows, pairs.T)

    me_g = lax.axis_index("grp")

    def word(own, cell, code, valid):
        x, y, z = code // 9, code // 3 % 3, code % 3
        return own | (cell << 3) | (code << 10) | (x << 15) | (y << 17) | (z << 19) | (
            valid.astype(jnp.int32) << 21
        )

    home = word(
        pairs[:, 0],
        ((1 + pairs[:, 1]) * n_grp + pairs[:, 2]) * cells + pairs[:, 3],
        pairs[:, 4],
        jnp.ones((listed,), jnp.bool_),
    )
    far_rows = far_rows.astype(jnp.int32)
    tiles = far_rows[:, 8:, :LANES].reshape(-1)
    seen = far_rows[: 2 * n_grp]
    slot = lax.broadcasted_iota(jnp.int32, (2 * n_grp, listed), 0)
    seen = seen[:, :, :listed]
    ours = (seen[:, 2] == me_g) & (seen[:, 1] == jnp.where(slot < n_grp, 1, 0))
    away = word(seen[:, 3], slot * cells + seen[:, 0], seen[:, 4], ours)
    ids = jnp.arange(cells, dtype=jnp.int32)
    alone = word(ids, (n_grp + me_g) * cells + ids, jnp.full((cells,), 13, jnp.int32), ids >= 0)
    words = jnp.concatenate([home, alone, away.reshape(-1)])
    words = jnp.pad(words, (0, -words.shape[0] % 8))
    n_words = words.shape[0]
    far = far.reshape(slots * (cells + 1), 8, width)
    tiled = width // LANES

    rho_act, rho_col, press_col, state, units, count = pl.pallas_call(
        density_kernel,
        out_shape=(
            shape((cells, picked)),
            shape((cells, picked, 1)),
            shape((cells, picked, 1)),
            shape((cells, width)),
            shape((n_words * tiled * groups + 8 + BATCH,), jnp.int32),
            shape((1,), jnp.int32),
        ),
        in_specs=[SMEM] * 3 + [VMEM] * 5,
        out_specs=(VMEM, VMEM, VMEM, VMEM, SMEM, SMEM),
        scratch_shapes=[
            pltpu.SMEM((n_words + 8,), jnp.int32),
            pltpu.SMEM((n_words * tiled + 8,), jnp.int32),
            pltpu.VMEM((4, cells * groups, 8, LANES), jnp.float32),
            pltpu.VMEM((cells * groups, 8, LANES), jnp.float32),
        ],
        compiler_params=pltpu.CompilerParams(vmem_limit_bytes=limit),
    )(words, mask.reshape(-1), tiles, far, act, arow, rank, own)

    far_state = pl.pallas_call(
        functools.partial(second_kernel, n_cells, n_grp),
        out_shape=shape((slots, cells, width)),
        in_specs=[VMEM],
        out_specs=ANY,
        scratch_shapes=[
            pltpu.SemaphoreType.DMA((n_copies,)),
            pltpu.SemaphoreType.DMA((n_copies,)),
            pltpu.SemaphoreType.DMA((1,)),
        ],
        compiler_params=pltpu.CompilerParams(collective_id=1, has_side_effects=True),
    )(state)

    acceleration = pl.pallas_call(
        force_kernel,
        out_shape=shape((3, cells, picked)),
        in_specs=[SMEM, SMEM] + [VMEM] * 6,
        out_specs=VMEM,
        scratch_shapes=[
            pltpu.VMEM((10, cells * groups, 8, LANES), jnp.float32),
            pltpu.VMEM((3, cells * groups, 8, LANES), jnp.float32),
            pltpu.VMEM((slots * cells, 8, width), jnp.float32),
        ],
        compiler_params=pltpu.CompilerParams(vmem_limit_bytes=limit),
    )(units, count, far, far_state, act, rho_col, press_col, rank)
    return rho_act, acceleration


def solution(mesh):
    split = ("cells", "grp")
    return jax.shard_map(
        local,
        mesh=mesh,
        in_specs=(
            P(None, split, None),
            P(None, split, None),
            P(split, None),
            P(split, None),
            P(split, None),
            P(split, None),
            P(split, None),
            P(split, None),
        ),
        out_specs=(P(split, None), P(None, split, None)),
        check_vma=False,
    )
```
